128 devices in a mesh: row: 8 (over x, core), col: 16 (over y, z).
Axes of the slice: x: 4, y: 4, z: 4, core: 2. Of those that a mesh axis runs over, the one named last changes fastest.
Arguments:
- p_valence: bfloat16 [4096, 4096], P('row', 'col'), as said below
- p_conduction: bfloat16 [4096, 4096], P('row', 'col'), as said below
- trial_vectors: bfloat16 [2, 4096, 4096], P(None, 'row', 'col'), may hold values from -6 to 6
- mask_valence: int32 [32, 32], replicated, may hold values from 0 to 1, as said below
- mask_conduction: int32 [32, 32], replicated, may hold values from 0 to 1, as said below
- mask_trial: int32 [32, 32], replicated, may hold values 0 or 1
- orbitals: bfloat16 [32, 128, 8192], P('row'), may hold values from -0.29882812 to 0.29882812
- sphere_starts: int32 [32], replicated, may hold values from 0 to 112, as said below
Outputs:
- kernel: bfloat16 [2, 4096, 4096], P(None, 'row', 'col')
- density: float32 [2, 65536], P(None, ('row', 'col'))
The draws below stay inside these ranges and needn't reach their ends.
Inputs may be any that keep to these rules, and one draw needn't show every extreme that they name: `mask_valence`: symmetric, ones on the block diagonal and next to it. `mask_conduction`: symmetric, ones on the block diagonal and next to it. `p_valence`: symmetric. `p_conduction`: symmetric. `sphere_starts`: the first block's start is 0 and the last block's 128 - 16.
All inputs are finite; a program needn't handle non-finite values.
Results may differ from the reference program's by a relative error of at most 0.0049.
Values may be sent and summed in bfloat16 or wider, within the bound.
No kernel may reach another device: no remote copies, remote signals or barrier semaphores. Data moves between devices by JAX's collectives and lax.ppermute only.
A program may use at most 192 MiB of HBM per device.

```python
import math
import jax
import jax.numpy as jnp
from jax import lax

BS = 128
NB = 32
SPAN = 16
SP = 512
NVEC = 2
NO = 4096
NSLAB = 128
N_ROW = 8
N_COL = 16


def symmetric_values(key):
    scale = 1.0 / math.sqrt(BS * (3.0 + (NB - 3) / 4.0))
    base = jax.random.normal(key, (NB * BS, NB * BS), jnp.float32)
    return ((base + base.T) * (scale * 0.70710678)).astype(jnp.bfloat16)


def symmetric_mask(key):
    coins = jax.random.randint(key, (NB, NB), 0, 4)
    chosen = coins == 0
    indices = jnp.arange(NB)
    banded = jnp.abs(indices[:, None] - indices[None, :]) <= 1
    return (chosen | chosen.T | banded).astype(jnp.int32)


def draw_p_valence(key, part):
    return symmetric_values(jax.random.fold_in(key, 11))


def draw_p_conduction(key, part):
    return symmetric_values(jax.random.fold_in(key, 12))


def draw_mask_valence(key, part):
    return symmetric_mask(jax.random.fold_in(key, 21))


def draw_mask_conduction(key, part):
    return symmetric_mask(jax.random.fold_in(key, 22))


def draw_sphere_starts(key, part):
    last_start = NSLAB - SPAN
    per_row = NB // N_ROW
    half_rows = max(N_ROW // 2, 1)
    stride = max(NSLAB // 2 // per_row, 1)
    indices = jnp.arange(NB, dtype=jnp.int32)
    placed = indices // per_row % half_rows * N_COL + indices % per_row * stride
    jitter = jax.random.randint(jax.random.fold_in(key, 31), (NB,), -2, 3)
    placed = jnp.clip(placed + jitter, 0, last_start)
    placed = placed.at[0].set(0).at[NB - 1].set(last_start)
    return placed.astype(jnp.int32)


def place_ends(entries, own_key, smallest, top_value):
    extent = entries.shape
    index_at = [jax.random.randint(jax.random.fold_in(own_key, axis), (), 0, extent[axis]) for axis in range(len(extent))]
    entries = entries.at[tuple(index_at)].set(smallest)
    longest = extent.index(max(extent))
    index_at[longest] = (index_at[longest] + 1) % extent[longest]
    return entries.at[tuple(index_at)].set(top_value)


def block_scale(key, extent, split, smallest, top_value):
    def one(position, blocks):
        draws = jax.random.uniform(jax.random.fold_in(jax.random.fold_in(key, 6), position), (blocks,), jnp.float32, smallest / len(split), top_value / len(split))
        return jnp.repeat(jnp.exp(draws), extent[position] // blocks).reshape((-1,) + (1,) * (len(extent) - position - 1))

    level = one(*split[0])
    for cut in split[1:]:
        level = level * one(*cut)
    return level


def scatter_about(own_key, dims, scale, bound, pieces=(), held_as=jnp.bfloat16):
    result = scale * jax.random.normal(own_key, dims, jnp.float32)
    if pieces:
        result = result * block_scale(own_key, dims, pieces, -0.22, 0.18)
    return jnp.clip(result, -bound, bound).astype(held_as)


def setup_inputs(seed: int = 0) -> dict:
    keys = jax.random.split(jax.random.key(seed), 9)
    return {
        "p_valence": draw_p_valence(jax.random.fold_in(keys[8], 71), 0),
        "p_conduction": draw_p_conduction(jax.random.fold_in(keys[8], 71), 0),
        "trial_vectors": scatter_about(keys[2], (NVEC, NO, NO), 1.0, 6.0, ((1, 8), (2, 16))),
        "mask_valence": draw_mask_valence(jax.random.fold_in(keys[8], 71), 0),
        "mask_conduction": draw_mask_conduction(jax.random.fold_in(keys[8], 71), 0),
        "mask_trial": place_ends((jax.random.randint(keys[5], (NB, NB), 0, 3) < 1).astype(jnp.int32), jax.random.fold_in(keys[5], 1), 0, 1),
        "orbitals": scatter_about(keys[6], (NB, BS, SPAN * SP), 0.05, 0.29882812, ((0, 8),)),
        "sphere_starts": draw_sphere_starts(jax.random.fold_in(keys[8], 71), 0),
    }


def expand(block_mask):
    widened = jnp.repeat(block_mask, BS, axis=0)
    return jnp.repeat(widened, BS, axis=1).astype(jnp.bfloat16)


def reference(p_valence, p_conduction, trial_vectors, mask_valence, mask_conduction, mask_trial, orbitals, sphere_starts):
    valence = p_valence * expand(mask_valence)
    conduction = p_conduction * expand(mask_conduction)
    trial_mask = expand(mask_trial)
    trials = trial_vectors * trial_mask[None]
    response = jnp.einsum("vik,kj->vij", trials.astype(jnp.float32), conduction.astype(jnp.float32)).astype(jnp.bfloat16)
    kernel_sum = jnp.einsum("ik,vkj->vij", valence.astype(jnp.float32), response.astype(jnp.float32))
    kernel = (kernel_sum * trial_mask.astype(jnp.float32)[None]).astype(jnp.bfloat16)
    shaped = orbitals.reshape(NB, BS, SPAN, SP)
    padded = jnp.pad(shaped, ((0, 0), (0, 0), (SPAN, SPAN), (0, 0)))

    def take_frame(orbital_block, offset):
        return lax.dynamic_slice_in_dim(orbital_block, offset, SPAN, 1)

    def add_block(index, density_grid):
        index = index.astype(jnp.int32)
        own_start = lax.dynamic_slice_in_dim(sphere_starts, index, 1, 0)[0]
        offsets = jnp.clip(own_start - sphere_starts + SPAN, 0, 2 * SPAN).astype(jnp.int32)
        frames = jax.vmap(take_frame)(padded, offsets).reshape(NB, BS, SPAN * SP)
        kernel_rows = lax.dynamic_slice_in_dim(kernel, index * BS, BS, 1).reshape(NVEC, BS, NB, BS)
        applied = jnp.einsum("vmjn,jnp->vmp", kernel_rows.astype(jnp.float32), frames.astype(jnp.float32))
        own_values = lax.dynamic_slice_in_dim(orbitals, index, 1, 0)[0].astype(jnp.float32)
        contrib = jnp.sum(own_values[None] * applied, axis=1).reshape(NVEC, SPAN, SP)
        zero_index = jnp.zeros((), jnp.int32)
        current = lax.dynamic_slice(density_grid, (zero_index, own_start, zero_index), (NVEC, SPAN, SP))
        return lax.dynamic_update_slice(density_grid, current + contrib, (zero_index, own_start, zero_index))

    density_grid = lax.fori_loop(0, NB, add_block, jnp.zeros((NVEC, NSLAB, SP), jnp.float32))
    return kernel, density_grid.reshape(NVEC, NSLAB * SP)
```

```python
import jax
import jax.numpy as jnp
from jax import lax
from jax.experimental import pallas as pl
from jax.experimental.pallas import tpu as pltpu
from jax.sharding import PartitionSpec as P

BS = 128
NB = 32
SPAN = 16
SP = 512
NSLAB = 128
RING = 4
N_COL = 16
BF16 = jnp.bfloat16
F32 = jnp.float32
AXES = ("row", "col")


def place(x, core, y, z):
    return ((x % RING) * 2 + core) * N_COL + (y % RING) * RING + z % RING


def pairs(move):
    out = []
    for x in range(RING):
        for core in range(2):
            for y in range(RING):
                for z in range(RING):
                    target = move(x, core, y, z, 1 - 2 * core)
                    if target is not None:
                        out.append((place(x, core, y, z), place(*target)))
    return out


ALONG_X = pairs(lambda x, core, y, z, d: (x + d, core, y, z))
ALONG_Y = pairs(lambda x, core, y, z, d: (x, core, y + d, z))
ALONG_Z = pairs(lambda x, core, y, z, d: (x, core, y, z + d))
OTHER_CORE = pairs(lambda x, core, y, z, d: (x, 1 - core, y, z))
FROM_HOLDER = pairs(lambda x, core, y, z, d: (x, 1 - core, y, z) if x == y and core == z // 2 else None)


def hop(step):
    return pairs(lambda x, core, y, z, d: (x + d, core, y, z) if (d * (x - y)) % RING == step else None)


def send(value, route):
    return lax.ppermute(value, AXES, route)


def ring(value, route):
    held = [value]
    for _ in range(RING - 1):
        held.append(send(held[-1], route))
    return held


def plane_gather(piece, first, second):
    return ring(jnp.stack(ring(piece, first)), second)


def masked(values, block_mask, row_index, col_index):
    row_blocks, col_blocks = values.shape[0] // BS, values.shape[1] // BS
    tile_mask = lax.dynamic_slice(
        block_mask, (row_index * row_blocks, col_index * col_blocks), (row_blocks, col_blocks)
    ).astype(values.dtype)
    shaped = values.reshape(row_blocks, BS, col_blocks, BS)
    return (shaped * tile_mask[:, None, :, None]).reshape(values.shape)


def source(idx, half, h, g):
    step = 1 - 2 * idx[1]
    dy, dz = (h, g) if half == 0 else (g, h)
    return (idx[2] - step * dy) & 3, (idx[3] - step * dz) & 3


def response_kernel(idx, mask, *refs):
    t_refs, c_own, c_other, out, panel = refs[:8], refs[8], refs[9], refs[10], refs[11]
    x, core, row = idx[0], idx[1], idx[4]
    step = 1 - 2 * core
    for s in range(RING):
        panel[((x - step * s) & 3) * 2 + core] = c_own[s]
        panel[((x + step * s) & 3) * 2 + 1 - core] = c_other[s]
    first_lanes = lax.broadcasted_iota(jnp.int32, (BS, 2 * BS), 1) < BS
    for v in range(2):
        total = jnp.zeros((4 * BS, 2 * BS), F32)
        for h in range(RING):
            lefts, rights = [], []
            for g in range(RING):
                ys, zs = source(idx, v, h, g)
                col = ys * RING + zs
                rows = []
                for i in range(4):
                    at = (row * 4 + i) * NB + col * 2
                    scale = jnp.where(first_lanes, mask[at].astype(F32), mask[at + 1].astype(F32)).astype(BF16)
                    rows.append(t_refs[v * RING + h][g, i * BS:(i + 1) * BS, :] * scale)
                lefts.append(jnp.concatenate(rows, axis=0))
                half_rows = pl.multiple_of((zs & 1) * 2 * BS, 2 * BS)
                rights.append(panel[col // 2, pl.ds(half_rows, 2 * BS), :])
            total += jnp.dot(
                jnp.concatenate(lefts, axis=1), jnp.concatenate(rights, axis=0), preferred_element_type=F32
            )
        out[v] = total.astype(BF16)


def density_kernel(idx, mask, starts, *refs):
    v_refs, r_own, r_other = refs[:8], refs[8:12], refs[12:16]
    orb_hbm, near_hbm, far_hbm, k_out, d_out, r_panel, orb, partner, dens, sems = refs[16:]
    x, core, row, col = idx[0], idx[1], idx[4], idx[5]
    step = 1 - 2 * core
    copies = [
        pltpu.make_async_copy(orb_hbm, orb, sems.at[0]),
        pltpu.make_async_copy(near_hbm, partner.at[core], sems.at[1]),
        pltpu.make_async_copy(far_hbm, partner.at[1 - core], sems.at[2]),
    ]
    for copy in copies:
        copy.start()
    for s in range(RING):
        r_panel[((x - step * s) & 3) * 2 + core] = r_own[s][...]
        r_panel[((x + step * s) & 3) * 2 + 1 - core] = r_other[s][...]
    first_lanes = lax.broadcasted_iota(jnp.int32, (BS, 2 * BS), 1) < BS
    for half in range(2):
        totals = [jnp.zeros((2 * BS, 2 * BS), F32) for _ in range(2)]
        for h in range(RING):
            left = jnp.concatenate([v_refs[half * RING + h][g] for g in range(RING)], axis=1)
            for v in range(2):
                rights = []
                for g in range(RING):
                    ys, zs = source(idx, half, h, g)
                    half_rows = pl.multiple_of((zs & 1) * 2 * BS, 2 * BS)
                    rights.append(r_panel[(ys * RING + zs) // 2, v, pl.ds(half_rows, 2 * BS), :])
                totals[v] += jnp.dot(left, jnp.concatenate(rights, axis=0), preferred_element_type=F32)
        for v in range(2):
            for i in range(2):
                at = (row * 4 + half * 2 + i) * NB + col * 2
                scale = jnp.where(first_lanes, mask[at].astype(F32), mask[at + 1].astype(F32))
                begin = (half * 2 + i) * BS
                k_out[v, begin:begin + BS, :] = (totals[v][i * BS:(i + 1) * BS] * scale).astype(BF16)
    dens[...] = jnp.zeros_like(dens)
    for copy in copies:
        copy.wait()
    starts_j = [starts[col * 2 + j] for j in range(2)]
    for i in range(4):
        left = jnp.concatenate([k_out[v, i * BS:(i + 1) * BS, :] for v in range(2)], axis=0)
        start_i = starts[row * 4 + i]

        def slab(s, carry, left=left, start_i=start_i, i=i):
            offsets = [start_i + s - starts_j[j] for j in range(2)]
            inside = [(o >= 0) & (o < SPAN) for o in offsets]

            @pl.when(inside[0] | inside[1])
            def _():
                frames = []
                for j in range(2):
                    at = pl.multiple_of(jnp.clip(offsets[j], 0, SPAN - 1) * SP, SP)
                    frame = partner[j, :, pl.ds(at, SP)]
                    frames.append(frame * jnp.where(inside[j], 1.0, 0.0).astype(BF16))
                applied = jnp.dot(left, jnp.concatenate(frames, axis=0), preferred_element_type=F32)
                own = orb[i, :, pl.ds(pl.multiple_of(s * SP, SP), SP)].astype(F32)
                for v in range(2):
                    terms = jnp.sum(own * applied[v * BS:(v + 1) * BS], axis=0, keepdims=True)
                    dens[pl.ds(start_i + s, 1), v * SP:(v + 1) * SP] += terms

            return carry

        lax.fori_loop(0, SPAN, slab, 0)
    d_out[...] = dens[...]


SMEM = pl.BlockSpec(memory_space=pltpu.SMEM)
VMEM = pl.BlockSpec(memory_space=pltpu.VMEM)
ANY = pl.BlockSpec(memory_space=pl.ANY)


def local(p_valence, p_conduction, trial_vectors, mask_valence, mask_conduction, mask_trial, orbitals, sphere_starts):
    row, col = lax.axis_index("row"), lax.axis_index("col")
    x, core, y, z = row // 2, row % 2, col // RING, col % RING
    idx = jnp.stack([x, core, y, z, row, col]).astype(jnp.int32)
    mask_flat = mask_trial.reshape(-1)

    trials = plane_gather(trial_vectors[0], ALONG_Z, ALONG_Y) + plane_gather(trial_vectors[1], ALONG_Y, ALONG_Z)
    conduction = masked(p_conduction, mask_conduction, row, col)
    c_own = jnp.stack(ring(conduction, ALONG_X))
    c_other = send(c_own, OTHER_CORE)

    valence = masked(p_valence, mask_valence, row, col)
    valences = plane_gather(valence[:2 * BS], ALONG_Z, ALONG_Y) + plane_gather(valence[2 * BS:], ALONG_Y, ALONG_Z)

    first = 2 * (col % 2)
    mine = lax.dynamic_slice_in_dim(orbitals, first + core, 1, 0)[0]
    theirs = lax.dynamic_slice_in_dim(orbitals, first + 1 - core, 1, 0)[0]
    given = send(theirs, FROM_HOLDER)
    seed = jnp.where(core == z // 2, mine, given)
    half_points = SPAN * SP // 2
    hops = (1 - 2 * core) * (x - y) % RING
    parts = []
    for k in range(2):
        held = seed[:, k * half_points:(k + 1) * half_points]
        kept = held
        for step in range(RING - 1):
            held = send(held, hop(step))
            kept = jnp.where(hops == step + 1, held, kept)
        parts.append(kept)
    near = jnp.concatenate(parts, axis=1)
    far = send(near, OTHER_CORE)

    response = pl.pallas_call(
        response_kernel,
        name="response",
        out_shape=jax.ShapeDtypeStruct((2, 4 * BS, 2 * BS), BF16),
        in_specs=[SMEM, SMEM] + [VMEM] * 10,
        out_specs=VMEM,
        scratch_shapes=[pltpu.VMEM((8, 4 * BS, 2 * BS), BF16)],
        compiler_params=pltpu.CompilerParams(vmem_limit_bytes=40 * 2**20),
        cost_estimate=pl.CostEstimate(flops=2**32, bytes_accessed=11 * 2**20, transcendentals=0),
    )(idx, mask_flat, *trials, c_own, c_other)

    r_own = ring(response, ALONG_X)
    r_other = [send(piece, OTHER_CORE) for piece in r_own]

    kernel, density = pl.pallas_call(
        density_kernel,
        name="density",
        out_shape=(
            jax.ShapeDtypeStruct((2, 4 * BS, 2 * BS), BF16),
            jax.ShapeDtypeStruct((NSLAB, 2 * SP), F32),
        ),
        in_specs=[SMEM, SMEM, SMEM] + [VMEM] * 16 + [ANY] * 3,
        out_specs=(VMEM, VMEM),
        scratch_shapes=[
            pltpu.VMEM((8, 2, 4 * BS, 2 * BS), BF16),
            pltpu.VMEM((4, BS, SPAN * SP), BF16),
            pltpu.VMEM((2, BS, SPAN * SP), BF16),
            pltpu.VMEM((NSLAB, 2 * SP), F32),
            pltpu.SemaphoreType.DMA((3,)),
        ],
        compiler_params=pltpu.CompilerParams(vmem_limit_bytes=48 * 2**20),
        cost_estimate=pl.CostEstimate(flops=2**33, bytes_accessed=22 * 2**20, transcendentals=0),
    )(idx, mask_flat, sphere_starts, *valences, *r_own, *r_other, orbitals, near, far)

    terms = lax.all_to_all(density, AXES, 0, 0, tiled=True)
    return kernel, jnp.sum(terms, axis=0).reshape(2, SP)


def solution(mesh):
    placed = (
        P("row", "col"),
        P("row", "col"),
        P(None, "row", "col"),
        P(),
        P(),
        P(),
        P("row", None, None),
        P(),
    )
    return jax.shard_map(
        local,
        mesh=mesh,
        in_specs=placed,
        out_specs=(P(None, "row", "col"), P(None, AXES)),
        check_vma=False,
    )
```

```python
import functools

import jax
import jax.numpy as jnp
from jax import lax
from jax.experimental import pallas as pl
from jax.experimental.pallas import tpu as pltpu
from jax.sharding import PartitionSpec as P

BS = 128
NB = 32
SPAN = 16
SP = 512
NSLAB = 128
RING = 4
N_COL = 16
BF16 = jnp.bfloat16
F32 = jnp.float32
AXES = ("row", "col")


def place(x, core, y, z):
    return ((x % RING) * 2 + core) * N_COL + (y % RING) * RING + z % RING


def pairs(move):
    out = []
    for x in range(RING):
        for core in range(2):
            for y in range(RING):
                for z in range(RING):
                    target = move(x, core, y, z)
                    if target is not None:
                        out.append((place(x, core, y, z), place(*target)))
    return out


def along(axis, step):
    def move(x, core, y, z, flip):
        at = [x, y, z]
        at["xyz".index(axis)] ^= flip
        return at[0], core, at[1], at[2]

    return pairs(lambda x, core, y, z: move(x, core, y, z, 1 if core == step else 3))


OTHER_CORE = pairs(lambda x, core, y, z: (x, 1 - core, y, z))

def send(value, route):
    return lax.ppermute(value, AXES, route)


def together(*values):
    return lax.optimization_barrier(values)


def masked(values, block_mask, row_index, col_index):
    row_blocks, col_blocks = values.shape[0] // BS, values.shape[1] // BS
    tile_mask = lax.dynamic_slice(
        block_mask, (row_index * row_blocks, col_index * col_blocks), (row_blocks, col_blocks)
    ).astype(values.dtype)
    shaped = values.reshape(row_blocks, BS, col_blocks, BS)
    return (shaped * tile_mask[:, None, :, None]).reshape(values.shape)


def offset(core, g):
    return (0, 1 + 2 * core, 3 - 2 * core, 2)[g]


def source(idx, first, h, g):
    dy, dz = (h, g) if first == 0 else (g, h)
    return idx[2] ^ offset(idx[1], dy), idx[3] ^ offset(idx[1], dz)


def piece_scale(mask, row_block, col_block, rows, dtype):
    first_lanes = lax.broadcasted_iota(jnp.int32, (BS, 2 * BS), 1) < BS
    scales = []
    for i in range(rows):
        at = (row_block + i) * NB + col_block
        scales.append(jnp.where(first_lanes, mask[at].astype(F32), mask[at + 1].astype(F32)).astype(dtype))
    return jnp.concatenate(scales, axis=0)


def group_left(idx, mask, ref, first, h, row_block):
    lefts = []
    for g in range(RING):
        ys, zs = source(idx, first, h, g)
        scale = piece_scale(mask, row_block, (ys * RING + zs) * 2, 2, BF16)
        lefts.append(ref[h % 2 * RING + g] * scale)
    return jnp.concatenate(lefts, axis=1)


def group_right(idx, panel, first, h, *lead):
    rights = []
    for g in range(RING):
        ys, zs = source(idx, first, h, g)
        half_rows = pl.multiple_of((zs & 1) * 2 * BS, 2 * BS)
        rights.append(panel[((ys * RING + zs) // 2, *lead, pl.ds(half_rows, 2 * BS))])
    return jnp.concatenate(rights, axis=0)


def response_kernel(part, idx, mask, *refs):
    t_refs, c_own, c_other = refs[:4], refs[4], refs[5]
    before, out, panel = (None, *refs[6:]) if part == 0 else refs[6:]
    x, core, row = idx[0], idx[1], idx[4]
    for g in range(RING):
        panel[(x ^ offset(core, g)) * 2 + core] = c_own[g]
        panel[(x ^ offset(1 - core, g)) * 2 + 1 - core] = c_other[g]
    for v in range(2):
        rights = [group_right(idx, panel, v, 2 * part + h) for h in range(2)]
        for half in range(2):
            rows = pl.ds(half * 2 * BS, 2 * BS)
            total = jnp.zeros((2 * BS, 2 * BS), F32) if part == 0 else before[v, rows]
            for h in range(2):
                left = group_left(idx, mask, t_refs[2 * half + v], v, 2 * part + h, row * 4 + half * 2)
                total += jnp.dot(left, rights[h], preferred_element_type=F32)
            out[v, rows] = total.astype(out.dtype)


def density_kernel(idx, mask, mask_v, starts, *refs):
    v_refs, r_refs = refs[:4], refs[4:10]
    orb_hbm, near_hbm, far_hbm, k_out, d_out, r_panel, orb, partner, dens, sems = refs[10:]
    x, core, row, col = idx[0], idx[1], idx[4], idx[5]
    copies = [
        pltpu.make_async_copy(orb_hbm, orb, sems.at[0]),
        pltpu.make_async_copy(near_hbm, partner.at[core], sems.at[1]),
        pltpu.make_async_copy(far_hbm, partner.at[1 - core], sems.at[2]),
    ]
    for copy in copies:
        copy.start()
    for side in range(2):
        own = core ^ side
        first, second, rest = r_refs[3 * side:3 * side + 3]
        r_panel[x * 2 + own] = first[...]
        r_panel[(x ^ offset(own, 1)) * 2 + own] = second[...]
        r_panel[(x ^ offset(own, 2)) * 2 + own] = rest[0]
        r_panel[(x ^ offset(own, 3)) * 2 + own] = rest[1]
    for half in range(2):
        totals = [jnp.zeros((2 * BS, 2 * BS), F32) for _ in range(2)]
        for h in range(RING):
            left = group_left(idx, mask_v, v_refs[half * 2 + h // 2], half, h, row * 4 + half * 2)
            for v in range(2):
                totals[v] += jnp.dot(left, group_right(idx, r_panel, half, h, v), preferred_element_type=F32)
        scale = piece_scale(mask, row * 4 + half * 2, col * 2, 2, F32)
        for v in range(2):
            k_out[v, half * 2 * BS:(half + 1) * 2 * BS, :] = (totals[v] * scale).astype(BF16)
    dens[...] = jnp.zeros_like(dens)
    for copy in copies:
        copy.wait()
    starts_j = [starts[col * 2 + j] for j in range(2)]
    for i in range(4):
        left = jnp.concatenate([k_out[v, i * BS:(i + 1) * BS, :] for v in range(2)], axis=0)
        start_i = starts[row * 4 + i]

        def slab(s, carry, left=left, start_i=start_i, i=i):
            offsets = [start_i + s - starts_j[j] for j in range(2)]
            inside = [(o >= 0) & (o < SPAN) for o in offsets]

            @pl.when(inside[0] | inside[1])
            def _():
                frames = []
                for j in range(2):
                    at = pl.multiple_of(jnp.clip(offsets[j], 0, SPAN - 1) * SP, SP)
                    frame = partner[j, :, pl.ds(at, SP)]
                    frames.append(frame * jnp.where(inside[j], 1.0, 0.0).astype(BF16))
                applied = jnp.dot(left, jnp.concatenate(frames, axis=0), preferred_element_type=F32)
                own = orb[i, :, pl.ds(pl.multiple_of(s * SP, SP), SP)].astype(F32)
                for v in range(2):
                    terms = jnp.sum(own * applied[v * BS:(v + 1) * BS], axis=0, keepdims=True)
                    dens[pl.ds(start_i + s, 1), v * SP:(v + 1) * SP] += terms

            return carry

        lax.fori_loop(0, SPAN, slab, 0)
    d_out[...] = dens[...]


SMEM = pl.BlockSpec(memory_space=pltpu.SMEM)
VMEM = pl.BlockSpec(memory_space=pltpu.VMEM)
ANY = pl.BlockSpec(memory_space=pl.ANY)


def local(p_valence, p_conduction, trial_vectors, mask_valence, mask_conduction, mask_trial, orbitals, sphere_starts):
    row, col = lax.axis_index("row"), lax.axis_index("col")
    x, core, y, z = row // 2, row % 2, col // RING, col % RING
    idx = jnp.stack([x, core, y, z, row, col]).astype(jnp.int32)
    mask_flat = mask_trial.reshape(-1)

    first = 2 * (col % 2)
    mine = lax.dynamic_slice_in_dim(orbitals, first + core, 1, 0)[0]
    theirs = lax.dynamic_slice_in_dim(orbitals, first + 1 - core, 1, 0)[0]

    by_z = jnp.concatenate([trial_vectors[0], p_valence[:2 * BS]])[None]
    by_y = jnp.concatenate([trial_vectors[1], p_valence[2 * BS:]])[None]
    by_x = masked(p_conduction, mask_conduction, row, col)[None]
    for step in range(2):
        outs = [send(by_z, along("z", step)), send(by_y, along("y", step)), send(by_x, along("x", step))]
        if step == 0:
            outs.append(send(theirs, OTHER_CORE))
        outs = together(*outs)
        if step == 0:
            given = outs[3]
        else:
            outs = together(*outs, given)
            given = outs[3]
        by_z, by_y, by_x = (jnp.concatenate(both) for both in zip((by_z, by_y, by_x), outs))
    seed = jnp.where(core == z // 2, mine, given)

    def across_plane(lo, hi):
        held = [by_z[:, lo:hi], by_y[:, lo:hi]]
        got = [send(held[0], along("y", 0)), send(held[1], along("z", 0))]
        near = [jnp.concatenate(both) for both in zip(held, got)]
        return near, [send(near[0], along("y", 1)), send(near[1], along("z", 1))]

    c_other = send(by_x, OTHER_CORE)
    upper, lower = across_plane(0, 2 * BS), across_plane(2 * BS, 4 * BS)
    reached = send(seed, along("x", 0))
    passed = jnp.where(x == y, seed, reached)

    response = None
    for part in range(2):
        last = part == 1
        response = pl.pallas_call(
            functools.partial(response_kernel, part),
            name="response",
            out_shape=jax.ShapeDtypeStruct((2, 4 * BS, 2 * BS), BF16 if last else F32),
            in_specs=[SMEM, SMEM] + [VMEM] * (7 if last else 6),
            out_specs=VMEM,
            scratch_shapes=[pltpu.VMEM((8, 4 * BS, 2 * BS), BF16)],
            compiler_params=pltpu.CompilerParams(vmem_limit_bytes=32 * 2**20),
            cost_estimate=pl.CostEstimate(flops=2**31, bytes_accessed=7 * 2**20, transcendentals=0),
        )(idx, mask_flat, *upper[part], *lower[part], by_x, c_other, *([response] if last else []))

    held, got, *upper_far = together(by_z[:, 4 * BS:], by_y[:, 4 * BS:], *upper[1])
    spread_out = send(passed, along("x", 1))
    outs = together(
        send(held, along("y", 0)),
        send(got, along("z", 0)),
        send(response, along("x", 0)),
        send(response, OTHER_CORE),
    )
    valence_0, valence_1 = jnp.concatenate([held, outs[0]]), jnp.concatenate([got, outs[1]])
    second, r_swapped = outs[2], outs[3]
    rest = send(jnp.stack([response, second]), along("x", 1))
    second_swapped = send(second, OTHER_CORE)
    valence_0_far, valence_1_far = send(valence_0, along("y", 1)), send(valence_1, along("z", 1))
    flip = 1 + 2 * core
    near = jnp.where((x == y) | (x ^ flip == y), passed, spread_out)
    far = send(near, OTHER_CORE)
    rest_swapped = send(rest, OTHER_CORE)
    valences = [valence_0, valence_0_far, valence_1, valence_1_far]
    responses = [response, second, rest, r_swapped, second_swapped, rest_swapped]

    kernel, density = pl.pallas_call(
        density_kernel,
        name="density",
        out_shape=(
            jax.ShapeDtypeStruct((2, 4 * BS, 2 * BS), BF16),
            jax.ShapeDtypeStruct((NSLAB, 2 * SP), F32),
        ),
        in_specs=[SMEM] * 4 + [VMEM] * 10 + [ANY] * 3,
        out_specs=(VMEM, VMEM),
        scratch_shapes=[
            pltpu.VMEM((8, 2, 4 * BS, 2 * BS), BF16),
            pltpu.VMEM((4, BS, SPAN * SP), BF16),
            pltpu.VMEM((2, BS, SPAN * SP), BF16),
            pltpu.VMEM((NSLAB, 2 * SP), F32),
            pltpu.SemaphoreType.DMA((3,)),
        ],
        compiler_params=pltpu.CompilerParams(vmem_limit_bytes=48 * 2**20),
        cost_estimate=pl.CostEstimate(flops=2**33, bytes_accessed=22 * 2**20, transcendentals=0),
    )(idx, mask_flat, mask_valence.reshape(-1), sphere_starts, *valences, *responses, orbitals, near, far)

    terms = lax.all_to_all(density, AXES, 0, 0, tiled=True)
    return kernel, jnp.sum(terms, axis=0).reshape(2, SP)


def solution(mesh):
    placed = (
        P("row", "col"),
        P("row", "col"),
        P(None, "row", "col"),
        P(),
        P(),
        P(),
        P("row", None, None),
        P(),
    )
    return jax.shard_map(
        local,
        mesh=mesh,
        in_specs=placed,
        out_specs=(P(None, "row", "col"), P(None, AXES)),
        check_vma=False,
    )
```

```python
import functools

import jax
import jax.numpy as jnp
from jax import lax
from jax.experimental import pallas as pl
from jax.experimental.pallas import tpu as pltpu
from jax.sharding import PartitionSpec as P

BS = 128
NB = 32
SPAN = 16
SP = 512
NSLAB = 128
RING = 4
N_COL = 16
WIDE = 2
BF16 = jnp.bfloat16
F32 = jnp.float32
AXES = ("row", "col")


def place(x, core, y, z):
    return ((x % RING) * 2 + core) * N_COL + (y % RING) * RING + z % RING


def pairs(move):
    out = []
    for x in range(RING):
        for core in range(2):
            for y in range(RING):
                for z in range(RING):
                    target = move(x, core, y, z)
                    if target is not None:
                        out.append((place(x, core, y, z), place(*target)))
    return out


def along(axis, step):
    def move(x, core, y, z, flip):
        at = [x, y, z]
        at["xyz".index(axis)] ^= flip
        return at[0], core, at[1], at[2]

    return pairs(lambda x, core, y, z: move(x, core, y, z, 1 if core == step else 3))


OTHER_CORE = pairs(lambda x, core, y, z: (x, 1 - core, y, z))

def send(value, route):
    return lax.ppermute(value, AXES, route)


def together(*values):
    return lax.optimization_barrier(values)


def masked(values, block_mask, row_index, col_index):
    row_blocks, col_blocks = values.shape[0] // BS, values.shape[1] // BS
    tile_mask = lax.dynamic_slice(
        block_mask, (row_index * row_blocks, col_index * col_blocks), (row_blocks, col_blocks)
    ).astype(values.dtype)
    shaped = values.reshape(row_blocks, BS, col_blocks, BS)
    return (shaped * tile_mask[:, None, :, None]).reshape(values.shape)


def offset(core, g):
    return (0, 1 + 2 * core, 3 - 2 * core, 2)[g]


def source(idx, first, h, g):
    dy, dz = (h, g) if first == 0 else (g, h)
    return idx[2] ^ offset(idx[1], dy), idx[3] ^ offset(idx[1], dz)


def piece_scale(mask, row_block, col_block, rows, dtype):
    first_lanes = lax.broadcasted_iota(jnp.int32, (BS, 2 * BS), 1) < BS
    scales = []
    for i in range(rows):
        at = (row_block + i) * NB + col_block
        scales.append(jnp.where(first_lanes, mask[at].astype(F32), mask[at + 1].astype(F32)).astype(dtype))
    return jnp.concatenate(scales, axis=0)


def group_left(idx, mask, ref, first, h, row_block):
    lefts = []
    for g in range(RING):
        ys, zs = source(idx, first, h, g)
        scale = piece_scale(mask, row_block, (ys * RING + zs) * 2, 2, BF16)
        lefts.append(ref[h % 2 * RING + g] * scale)
    return jnp.concatenate(lefts, axis=1)


def group_right(idx, panel, first, h, *lead):
    rights = []
    for g in range(RING):
        ys, zs = source(idx, first, h, g)
        half_rows = pl.multiple_of((zs & 1) * 2 * BS, 2 * BS)
        rights.append(panel[((ys * RING + zs) // 2, *lead, pl.ds(half_rows, 2 * BS))])
    return jnp.concatenate(rights, axis=0)


def response_kernel(part, idx, mask, *refs):
    t_refs, c_own, c_other = refs[:4], refs[4], refs[5]
    before, out, panel = (None, *refs[6:]) if part == 0 else refs[6:]
    x, core, row = idx[0], idx[1], idx[4]
    for g in range(RING):
        panel[(x ^ offset(core, g)) * 2 + core] = c_own[g]
        panel[(x ^ offset(1 - core, g)) * 2 + 1 - core] = c_other[g]
    for v in range(2):
        rights = [group_right(idx, panel, v, 2 * part + h) for h in range(2)]
        for half in range(2):
            rows = pl.ds(half * 2 * BS, 2 * BS)
            total = jnp.zeros((2 * BS, 2 * BS), F32) if part == 0 else before[v, rows]
            for h in range(2):
                left = group_left(idx, mask, t_refs[2 * half + v], v, 2 * part + h, row * 4 + half * 2)
                total += jnp.dot(left, rights[h], preferred_element_type=F32)
            out[v, rows] = total.astype(out.dtype)


def density_kernel(idx, mask, mask_v, starts, *refs):
    v_refs, r_refs = refs[:4], refs[4:10]
    orb_hbm, near_hbm, far_hbm, k_out, dens, r_panel, orb, partner, sems = refs[10:]
    x, core, row, col = idx[0], idx[1], idx[4], idx[5]
    copies = [(near_hbm, partner.at[core]), (far_hbm, partner.at[1 - core])]
    copies += [(orb_hbm.at[i], orb.at[i]) for i in range(4)]
    copies = [pltpu.make_async_copy(a, b, sems.at[k]) for k, (a, b) in enumerate(copies)]
    for copy in copies:
        copy.start()
    for side in range(2):
        own = core ^ side
        first, second, rest = r_refs[3 * side:3 * side + 3]
        r_panel[x * 2 + own] = first[...]
        r_panel[(x ^ offset(own, 1)) * 2 + own] = second[...]
        r_panel[(x ^ offset(own, 2)) * 2 + own] = rest[0]
        r_panel[(x ^ offset(own, 3)) * 2 + own] = rest[1]
    for half in range(2):
        totals = [jnp.zeros((2 * BS, 2 * BS), F32) for _ in range(2)]
        for h in range(RING):
            left = group_left(idx, mask_v, v_refs[half * 2 + h // 2], half, h, row * 4 + half * 2)
            for v in range(2):
                totals[v] += jnp.dot(left, group_right(idx, r_panel, half, h, v), preferred_element_type=F32)
        scale = piece_scale(mask, row * 4 + half * 2, col * 2, 2, F32)
        for v in range(2):
            k_out[v, half * 2 * BS:(half + 1) * 2 * BS, :] = (totals[v] * scale).astype(BF16)
    dens[...] = jnp.zeros_like(dens)
    copies[0].wait()
    copies[1].wait()
    starts_j = [starts[col * 2 + j] for j in range(2)]
    for i in range(4):
        copies[2 + i].wait()
        left = jnp.concatenate([k_out[v, i * BS:(i + 1) * BS, :] for v in range(2)], axis=0)
        start_i = starts[row * 4 + i]

        def slabs(step, carry, left=left, start_i=start_i, i=i):
            begin = step * WIDE
            offsets = [start_i + begin - starts_j[j] for j in range(2)]
            touched = [(o > -WIDE) & (o < SPAN) for o in offsets]

            @pl.when(touched[0] | touched[1])
            def _():
                for k in range(WIDE):
                    frames = []
                    for j in range(2):
                        o = offsets[j] + k
                        at = pl.multiple_of(jnp.clip(o, 0, SPAN - 1) * SP, SP)
                        inside = jnp.where((o >= 0) & (o < SPAN), 1.0, 0.0).astype(BF16)
                        frames.append(partner[j, :, pl.ds(at, SP)] * inside)
                    applied = jnp.dot(left, jnp.concatenate(frames, axis=0), preferred_element_type=F32)
                    own = orb[i, :, pl.ds(pl.multiple_of((begin + k) * SP, SP), SP)].astype(F32)
                    for v in range(2):
                        terms = jnp.sum(own * applied[v * BS:(v + 1) * BS], axis=0, keepdims=True)
                        for q in range(4):
                            dens[start_i + begin + k, pl.ds(v * 4 + q, 1), :] += terms[:, q * BS:(q + 1) * BS]

            return carry

        lax.fori_loop(0, SPAN // WIDE, slabs, 0)


SMEM = pl.BlockSpec(memory_space=pltpu.SMEM)
VMEM = pl.BlockSpec(memory_space=pltpu.VMEM)
ANY = pl.BlockSpec(memory_space=pl.ANY)


def local(p_valence, p_conduction, trial_vectors, mask_valence, mask_conduction, mask_trial, orbitals, sphere_starts):
    row, col = lax.axis_index("row"), lax.axis_index("col")
    x, core, y, z = row // 2, row % 2, col // RING, col % RING
    idx = jnp.stack([x, core, y, z, row, col]).astype(jnp.int32)
    mask_flat = mask_trial.reshape(-1)

    first = 2 * (col % 2)
    theirs = lax.dynamic_slice_in_dim(orbitals, first + 1 - core, 1, 0)[0]
    by_z = jnp.concatenate([trial_vectors[0], p_valence[:2 * BS]])[None]
    by_y = jnp.concatenate([trial_vectors[1], p_valence[2 * BS:]])[None]
    by_x = masked(p_conduction, mask_conduction, row, col)[None]
    z_got, y_got, x_got, given, first = together(
        send(by_z, along("z", 0)), send(by_y, along("y", 0)), send(by_x, along("x", 0)), send(theirs, OTHER_CORE), first
    )
    by_z, by_y, by_x = (jnp.concatenate(both) for both in ((by_z, z_got), (by_y, y_got), (by_x, x_got)))
    z_got, y_got, x_got, given, first = together(
        send(by_z, along("z", 1)), send(by_y, along("y", 1)), send(by_x, along("x", 1)), given, first
    )
    by_z, by_y, by_x = (jnp.concatenate(both) for both in ((by_z, z_got), (by_y, y_got), (by_x, x_got)))
    mine = lax.dynamic_slice_in_dim(orbitals, first + core, 1, 0)[0]
    seed = jnp.where(core == z // 2, mine, given)

    upper, lower = [by_z[:, :2 * BS], by_y[:, :2 * BS]], [by_z[:, 2 * BS:4 * BS], by_y[:, 2 * BS:4 * BS]]

    def first_step(held):
        return [send(held[0], along("y", 0)), send(held[1], along("z", 0))]

    def second_step(held, got):
        near = [jnp.concatenate(both) for both in zip(held, got)]
        return near, [send(near[0], along("y", 1)), send(near[1], along("z", 1))]

    upper = second_step(upper, first_step(upper))
    *lower_got, reached, by_x = together(*first_step(lower), send(seed, along("x", 0)), by_x)
    lower = second_step(lower, lower_got)
    c_other = send(by_x, OTHER_CORE)
    passed = jnp.where(x == y, seed, reached)
    arrived = send(passed, along("x", 1))

    response = None
    for part in range(2):
        last = part == 1
        if last:
            by_z, by_y, upper[1][0], upper[1][1] = together(by_z, by_y, *upper[1])
        response = pl.pallas_call(
            functools.partial(response_kernel, part),
            name="response",
            out_shape=jax.ShapeDtypeStruct((2, 4 * BS, 2 * BS), BF16 if last else F32),
            in_specs=[SMEM, SMEM] + [VMEM] * (7 if last else 6),
            out_specs=VMEM,
            scratch_shapes=[pltpu.VMEM((8, 4 * BS, 2 * BS), BF16)],
            compiler_params=pltpu.CompilerParams(vmem_limit_bytes=32 * 2**20),
            cost_estimate=pl.CostEstimate(flops=2**31, bytes_accessed=7 * 2**20, transcendentals=0),
        )(idx, mask_flat, *upper[part], *lower[part], by_x, c_other, *([response] if last else []))

    held, got = by_z[:, 4 * BS:], by_y[:, 4 * BS:]
    outs = together(
        send(held, along("y", 0)),
        send(got, along("z", 0)),
        send(response, along("x", 0)),
        send(response, OTHER_CORE),
    )
    valence_0, valence_1 = jnp.concatenate([held, outs[0]]), jnp.concatenate([got, outs[1]])
    second, r_swapped = outs[2], outs[3]
    rest = send(jnp.stack([response, second]), along("x", 1))
    second_swapped = send(second, OTHER_CORE)
    valence_0_far, valence_1_far = send(valence_0, along("y", 1)), send(valence_1, along("z", 1))
    flip = 1 + 2 * core
    arrived, second = together(arrived, second)
    near = jnp.where((x == y) | (x ^ flip == y), passed, arrived)
    far = send(near, OTHER_CORE)
    rest_swapped = send(rest, OTHER_CORE)
    valences = [valence_0, valence_0_far, valence_1, valence_1_far]
    responses = [response, second, rest, r_swapped, second_swapped, rest_swapped]

    kernel, density = pl.pallas_call(
        density_kernel,
        name="density",
        out_shape=(
            jax.ShapeDtypeStruct((2, 4 * BS, 2 * BS), BF16),
            jax.ShapeDtypeStruct((NSLAB, 8, BS), F32),
        ),
        in_specs=[SMEM] * 4 + [VMEM] * 10 + [ANY] * 3,
        out_specs=(VMEM, VMEM),
        scratch_shapes=[
            pltpu.VMEM((8, 2, 4 * BS, 2 * BS), BF16),
            pltpu.VMEM((4, BS, SPAN * SP), BF16),
            pltpu.VMEM((2, BS, SPAN * SP), BF16),
            pltpu.SemaphoreType.DMA((6,)),
        ],
        compiler_params=pltpu.CompilerParams(vmem_limit_bytes=48 * 2**20),
        cost_estimate=pl.CostEstimate(flops=2**33, bytes_accessed=22 * 2**20, transcendentals=0),
    )(idx, mask_flat, mask_valence.reshape(-1), sphere_starts, *valences, *responses, orbitals, near, far)

    terms = lax.all_to_all(density, AXES, 0, 0, tiled=True)
    return kernel, jnp.sum(terms, axis=0).reshape(2, SP)


def solution(mesh):
    placed = (
        P("row", "col"),
        P("row", "col"),
        P(None, "row", "col"),
        P(),
        P(),
        P(),
        P("row", None, None),
        P(),
    )
    return jax.shard_map(
        local,
        mesh=mesh,
        in_specs=placed,
        out_specs=(P(None, "row", "col"), P(None, AXES)),
        check_vma=False,
    )
```

```python
import functools

import jax
import jax.numpy as jnp
from jax import lax
from jax.experimental import pallas as pl
from jax.experimental.pallas import tpu as pltpu
from jax.sharding import PartitionSpec as P

BS = 128
NB = 32
SPAN = 16
SP = 512
NSLAB = 128
RING = 4
N_COL = 16
WIDE = 2
BF16 = jnp.bfloat16
F32 = jnp.float32
AXES = ("row", "col")


def place(x, core, y, z):
    return ((x % RING) * 2 + core) * N_COL + (y % RING) * RING + z % RING


def pairs(move):
    out = []
    for x in range(RING):
        for core in range(2):
            for y in range(RING):
                for z in range(RING):
                    target = move(x, core, y, z)
                    if target is not None:
                        out.append((place(x, core, y, z), place(*target)))
    return out


def along(axis, step):
    def move(x, core, y, z, flip):
        at = [x, y, z]
        at["xyz".index(axis)] ^= flip
        return at[0], core, at[1], at[2]

    return pairs(lambda x, core, y, z: move(x, core, y, z, 1 if core == step else 3))


OTHER_CORE = pairs(lambda x, core, y, z: (x, 1 - core, y, z))

def send(value, route):
    return lax.ppermute(value, AXES, route)


def together(*values):
    return lax.optimization_barrier(values)


def neighbours(value, axis):
    return [send(value, along(axis, 0)), send(value, along(axis, 1))]


def gather(value, axis):
    first, second = neighbours(value, axis)
    return [value, first, second, send(first, along(axis, 1))]


def masked(values, block_mask, row_index, col_index):
    row_blocks, col_blocks = values.shape[0] // BS, values.shape[1] // BS
    tile_mask = lax.dynamic_slice(
        block_mask, (row_index * row_blocks, col_index * col_blocks), (row_blocks, col_blocks)
    ).astype(values.dtype)
    shaped = values.reshape(row_blocks, BS, col_blocks, BS)
    return (shaped * tile_mask[:, None, :, None]).reshape(values.shape)


def offset(core, g):
    return (0, 1 + 2 * core, 3 - 2 * core, 2)[g]


def source(idx, first, h, g):
    dy, dz = (h, g) if first == 0 else (g, h)
    return idx[2] ^ offset(idx[1], dy), idx[3] ^ offset(idx[1], dz)


def place_of(core, flip):
    return jnp.where(flip == 2, 3, jnp.where(flip == 0, 0, jnp.where(flip == 1 + 2 * core, 1, 2)))


def piece_scale(mask, row_block, col_block, rows, dtype):
    first_lanes = lax.broadcasted_iota(jnp.int32, (BS, 2 * BS), 1) < BS
    scales = []
    for i in range(rows):
        at = (row_block + i) * NB + col_block
        scales.append(jnp.where(first_lanes, mask[at].astype(F32), mask[at + 1].astype(F32)).astype(dtype))
    return jnp.concatenate(scales, axis=0)


def half_rows(zs):
    return pl.ds(pl.multiple_of((zs & 1) * 2 * BS, 2 * BS), 2 * BS)


def response_kernel(part, idx, mask, *refs):
    groups = ((0, 1, 2), (3,))[part]
    count = 2 * len(groups)
    t_refs, c_own, c_other = refs[:count], refs[count], refs[count + 1]
    before, out, panel = (None, *refs[count + 2:]) if part == 0 else refs[count + 2:]
    x, core, row = idx[0], idx[1], idx[4]
    for g in range(RING):
        panel[(x ^ offset(core, g)) * 2 + core] = c_own[g]
        panel[(x ^ offset(1 - core, g)) * 2 + 1 - core] = c_other[g]
    for v in range(2):
        total = jnp.zeros((4 * BS, 2 * BS), F32) if part == 0 else before[v]
        for k, h in enumerate(groups):
            lefts, rights = [], []
            for g in range(RING):
                ys, zs = source(idx, v, h, g)
                col = ys * RING + zs
                lefts.append(t_refs[v * len(groups) + k][g] * piece_scale(mask, row * 4, col * 2, 4, BF16))
                rights.append(panel[col // 2, half_rows(zs), :])
            total += jnp.dot(
                jnp.concatenate(lefts, axis=1), jnp.concatenate(rights, axis=0), preferred_element_type=F32
            )
        out[v] = total.astype(out.dtype)


def kernel_terms(idx, mask_v, valence, r_panel, flips):
    x, core, z, row = idx[0], idx[1], idx[3], idx[4]
    totals = [[0.0, 0.0], [0.0, 0.0]]
    for slot, flip in enumerate(flips):
        ys = x ^ flip
        for half in range(2):
            lefts, places = [], []
            for g in range(RING):
                zs = z ^ offset(core, g)
                lefts.append(valence(half, ys, g) * piece_scale(mask_v, row * 4 + half * 2, (ys * RING + zs) * 2, 2, BF16))
                places.append(zs)
            left = jnp.concatenate(lefts, axis=1)
            for v in range(2):
                rights = [r_panel[slot * 2 + zs // 2, v, half_rows(zs), :] for zs in places]
                totals[half][v] += jnp.dot(left, jnp.concatenate(rights, axis=0), preferred_element_type=F32)
    return totals


def panel_copies(idx, v_refs, v_panel):
    out = [(v_refs[h], v_panel.at[0, idx[2] ^ offset(idx[1], h)]) for h in range(RING)]
    out += [(v_refs[RING + g], v_panel.at[1, g]) for g in range(RING)]
    return out


def start_all(copies, sems):
    copies = [pltpu.make_async_copy(a, b, sems.at[k]) for k, (a, b) in enumerate(copies)]
    for copy in copies:
        copy.start()
    return copies


def early_kernel(idx, mask_v, *refs):
    v_refs, r_refs, out, v_last, v_panel, r_panel, sems = refs[:8], refs[8:14], *refs[14:]
    core, y = idx[1], idx[2]
    copies = panel_copies(idx, v_refs, v_panel)
    for side in range(2):
        own = core ^ side
        copies.append((r_refs[3 * side], r_panel.at[own]))
        copies.append((r_refs[3 * side + 1], r_panel.at[(1 + own) * 2 + own]))
        copies.append((r_refs[3 * side + 2], r_panel.at[(2 - own) * 2 + own]))
    for copy in start_all(copies, sems):
        copy.wait()

    def valence(half, ys, g):
        return v_panel[0, ys, g] if half == 0 else v_panel[1, g, place_of(core, y ^ ys)]

    for half in range(2):
        for g in range(RING):
            v_last[half, g] = valence(half, idx[0] ^ 2, g)
    totals = kernel_terms(idx, mask_v, valence, r_panel, (0, 1, 3))
    for half in range(2):
        for v in range(2):
            out[v, half * 2 * BS:(half + 1) * 2 * BS, :] = totals[half][v]


def density_kernel(idx, mask, mask_v, starts, *refs):
    v_last, r_own, r_other, before, orb_hbm, near_hbm, far_hbm, k_out, dens, r_panel, orb, partner, sems = refs
    core, row, col = idx[1], idx[4], idx[5]
    copies = [(near_hbm, partner.at[core]), (far_hbm, partner.at[1 - core])]
    copies = start_all(copies + [(orb_hbm.at[i], orb.at[i]) for i in range(4)], sems)
    r_panel[core] = r_own[...]
    r_panel[1 - core] = r_other[...]
    totals = kernel_terms(idx, mask_v, lambda half, ys, g: v_last[half, g], r_panel, (2,))
    for half in range(2):
        scale = piece_scale(mask, row * 4 + half * 2, col * 2, 2, F32)
        rows = slice(half * 2 * BS, (half + 1) * 2 * BS)
        for v in range(2):
            k_out[v, rows, :] = ((before[v, rows, :] + totals[half][v]) * scale).astype(BF16)
    dens[...] = jnp.zeros_like(dens)
    copies[0].wait()
    copies[1].wait()
    starts_j = [starts[col * 2 + j] for j in range(2)]
    for i in range(4):
        copies[2 + i].wait()
        left = jnp.concatenate([k_out[v, i * BS:(i + 1) * BS, :] for v in range(2)], axis=0)
        start_i = starts[row * 4 + i]

        def slabs(step, carry, left=left, start_i=start_i, i=i):
            begin = step * WIDE
            offsets = [start_i + begin - starts_j[j] for j in range(2)]
            touched = [(o > -WIDE) & (o < SPAN) for o in offsets]

            @pl.when(touched[0] | touched[1])
            def _():
                for k in range(WIDE):
                    frames = []
                    for j in range(2):
                        o = offsets[j] + k
                        at = pl.multiple_of(jnp.clip(o, 0, SPAN - 1) * SP, SP)
                        inside = jnp.where((o >= 0) & (o < SPAN), 1.0, 0.0).astype(BF16)
                        frames.append(partner[j, :, pl.ds(at, SP)] * inside)
                    applied = jnp.dot(left, jnp.concatenate(frames, axis=0), preferred_element_type=F32)
                    own = orb[i, :, pl.ds(pl.multiple_of((begin + k) * SP, SP), SP)].astype(F32)
                    for v in range(2):
                        terms = jnp.sum(own * applied[v * BS:(v + 1) * BS], axis=0, keepdims=True)
                        for q in range(4):
                            dens[start_i + begin + k, pl.ds(v * 4 + q, 1), :] += terms[:, q * BS:(q + 1) * BS]

            return carry

        lax.fori_loop(0, SPAN // WIDE, slabs, 0)


SMEM = pl.BlockSpec(memory_space=pltpu.SMEM)
VMEM = pl.BlockSpec(memory_space=pltpu.VMEM)
ANY = pl.BlockSpec(memory_space=pl.ANY)


def local(p_valence, p_conduction, trial_vectors, mask_valence, mask_conduction, mask_trial, orbitals, sphere_starts):
    row, col = lax.axis_index("row"), lax.axis_index("col")
    x, core, y, z = row // 2, row % 2, col // RING, col % RING
    idx = jnp.stack([x, core, y, z, row, col]).astype(jnp.int32)
    mask_flat = mask_trial.reshape(-1)

    first = 2 * (col % 2)
    conduction = masked(p_conduction, mask_conduction, row, col)
    both_z = jnp.concatenate([trial_vectors[0], p_valence[:2 * BS]])
    both_y = jnp.concatenate([trial_vectors[1], p_valence[2 * BS:]])

    theirs = lax.dynamic_slice_in_dim(orbitals, first + 1 - core, 1, 0)[0]
    z_first, y_first, z_second, y_second, given, conduction, first = together(
        send(both_z, along("z", 0)), send(both_y, along("y", 0)),
        send(both_z, along("z", 1)), send(both_y, along("y", 1)),
        send(theirs, OTHER_CORE), conduction, first,
    )
    mine = lax.dynamic_slice_in_dim(orbitals, first + core, 1, 0)[0]
    seed = jnp.where(core == z // 2, mine, given)
    reached = send(seed, along("x", 0))
    z_third, y_third, x_first, x_second = together(
        send(z_first, along("z", 1)), send(y_first, along("y", 1)), *neighbours(conduction, "x")
    )
    by_z, by_y = [both_z, z_first, z_second, z_third], [both_y, y_first, y_second, y_third]
    own_0 = jnp.stack([piece[:4 * BS] for piece in by_z])
    own_1 = jnp.stack([piece[:4 * BS] for piece in by_y])
    *others, x_third = together(
        *neighbours(own_0, "y"), *neighbours(own_1, "z"), send(x_first, along("x", 1))
    )
    trials_0, trials_1 = [own_0] + others[:2], [own_1] + others[2:]
    trials_0.append(send(trials_0[1], along("y", 1)))
    trials_1.append(send(trials_1[1], along("z", 1)))
    c_own = jnp.stack([conduction, x_first, x_second, x_third])
    c_other = send(c_own, OTHER_CORE)
    passed = jnp.where(x == y, seed, reached)
    arrived = send(passed, along("x", 1))


    response = None
    for part in range(2):
        if part == 1:
            *ends, trials_0[3], trials_1[3], response = together(
                *[piece[4 * BS:] for piece in by_z + by_y], trials_0[3], trials_1[3], response
            )
        groups = (slice(0, 3), slice(3, 4))[part]
        pieces = trials_0[groups] + trials_1[groups]
        response = pl.pallas_call(
            functools.partial(response_kernel, part),
            name="response",
            out_shape=jax.ShapeDtypeStruct((2, 4 * BS, 2 * BS), (F32, BF16)[part]),
            in_specs=[SMEM, SMEM] + [VMEM] * (len(pieces) + 2 + part),
            out_specs=VMEM,
            scratch_shapes=[pltpu.VMEM((8, 4 * BS, 2 * BS), BF16)],
            compiler_params=pltpu.CompilerParams(vmem_limit_bytes=24 * 2**20),
            cost_estimate=pl.CostEstimate(flops=2**(32 + 4 * part), bytes_accessed=9 * 2**20, transcendentals=0),
        )(idx, mask_flat, *pieces, c_own, c_other, *([response] if part else []))

    valences = [jnp.stack(ends[:4]), jnp.stack(ends[4:8])]
    valences = [valences[0], send(valences[0], along("y", 0)), valences[1], send(valences[1], along("z", 0))]
    responses = gather(response, "x")
    valences[1], valences[3], *responses[1:3], arrived = together(valences[1], valences[3], *responses[1:3], arrived)
    for at, axis in ((0, "y"), (4, "z")):
        valences[at + 2:at + 2] = [send(valences[at], along(axis, 1)), send(valences[at + 1], along(axis, 1))]
    swapped = [send(piece, OTHER_CORE) for piece in responses]
    near = jnp.where((x == y) | (x ^ (1 + 2 * core) == y), passed, arrived)
    far = send(near, OTHER_CORE)
    mask_v = mask_valence.reshape(-1)

    early, v_last = pl.pallas_call(
        early_kernel,
        name="early",
        out_shape=(
            jax.ShapeDtypeStruct((2, 4 * BS, 2 * BS), F32),
            jax.ShapeDtypeStruct((2, RING, 2 * BS, 2 * BS), BF16),
        ),
        in_specs=[SMEM, SMEM] + [ANY] * 14,
        out_specs=(VMEM, VMEM),
        scratch_shapes=[
            pltpu.VMEM((2, RING, RING, 2 * BS, 2 * BS), BF16),
            pltpu.VMEM((6, 2, 4 * BS, 2 * BS), BF16),
            pltpu.SemaphoreType.DMA((14,)),
        ],
        compiler_params=pltpu.CompilerParams(vmem_limit_bytes=20 * 2**20),
        cost_estimate=pl.CostEstimate(flops=2**36, bytes_accessed=8 * 2**20, transcendentals=0),
    )(idx, mask_v, *valences, *responses[:3], *swapped[:3])

    kernel, density = pl.pallas_call(
        density_kernel,
        name="density",
        out_shape=(
            jax.ShapeDtypeStruct((2, 4 * BS, 2 * BS), BF16),
            jax.ShapeDtypeStruct((NSLAB, 8, BS), F32),
        ),
        in_specs=[SMEM] * 4 + [VMEM] * 4 + [ANY] * 3,
        out_specs=(VMEM, VMEM),
        scratch_shapes=[
            pltpu.VMEM((2, 2, 4 * BS, 2 * BS), BF16),
            pltpu.VMEM((4, BS, SPAN * SP), BF16),
            pltpu.VMEM((2, BS, SPAN * SP), BF16),
            pltpu.SemaphoreType.DMA((6,)),
        ],
        compiler_params=pltpu.CompilerParams(vmem_limit_bytes=28 * 2**20),
        cost_estimate=pl.CostEstimate(flops=2**33, bytes_accessed=22 * 2**20, transcendentals=0),
    )(idx, mask_flat, mask_v, sphere_starts, v_last, responses[3], swapped[3], early, orbitals, near, far)

    terms = lax.all_to_all(density, AXES, 0, 0, tiled=True)
    return kernel, jnp.sum(terms, axis=0).reshape(2, SP)


def solution(mesh):
    placed = (
        P("row", "col"),
        P("row", "col"),
        P(None, "row", "col"),
        P(),
        P(),
        P(),
        P("row", None, None),
        P(),
    )
    return jax.shard_map(
        local,
        mesh=mesh,
        in_specs=placed,
        out_specs=(P(None, "row", "col"), P(None, AXES)),
        check_vma=False,
    )
```

```python
import functools

import jax
import jax.numpy as jnp
from jax import lax
from jax.experimental import pallas as pl
from jax.experimental.pallas import tpu as pltpu
from jax.sharding import PartitionSpec as P

BS = 128
NB = 32
SPAN = 16
SP = 512
NSLAB = 128
RING = 4
N_COL = 16
WIDE = 2
BF16 = jnp.bfloat16
F32 = jnp.float32
AXES = ("row", "col")


def place(x, core, y, z):
    return ((x % RING) * 2 + core) * N_COL + (y % RING) * RING + z % RING


def pairs(move):
    out = []
    for x in range(RING):
        for core in range(2):
            for y in range(RING):
                for z in range(RING):
                    target = move(x, core, y, z)
                    if target is not None:
                        out.append((place(x, core, y, z), place(*target)))
    return out


def along(axis, step):
    def move(x, core, y, z, flip):
        at = [x, y, z]
        at["xyz".index(axis)] ^= flip
        return at[0], core, at[1], at[2]

    return pairs(lambda x, core, y, z: move(x, core, y, z, 1 if core == step else 3))


OTHER_CORE = pairs(lambda x, core, y, z: (x, 1 - core, y, z))

def send(value, route):
    return lax.ppermute(value, AXES, route)


def together(*values):
    return lax.optimization_barrier(values)


def neighbours(value, axis):
    return [send(value, along(axis, 0)), send(value, along(axis, 1))]


def gather(value, axis):
    first, second = neighbours(value, axis)
    return [value, first, second, send(first, along(axis, 1))]


def masked(values, block_mask, row_index, col_index):
    row_blocks, col_blocks = values.shape[0] // BS, values.shape[1] // BS
    tile_mask = lax.dynamic_slice(
        block_mask, (row_index * row_blocks, col_index * col_blocks), (row_blocks, col_blocks)
    ).astype(values.dtype)
    shaped = values.reshape(row_blocks, BS, col_blocks, BS)
    return (shaped * tile_mask[:, None, :, None]).reshape(values.shape)


def offset(core, g):
    return (0, 1 + 2 * core, 3 - 2 * core, 2)[g]


def source(idx, first, h, g):
    dy, dz = (h, g) if first == 0 else (g, h)
    return idx[2] ^ offset(idx[1], dy), idx[3] ^ offset(idx[1], dz)


def place_of(core, flip):
    return jnp.where(flip == 2, 3, jnp.where(flip == 0, 0, jnp.where(flip == 1 + 2 * core, 1, 2)))


def piece_scale(mask, row_block, col_block, rows, dtype):
    first_lanes = lax.broadcasted_iota(jnp.int32, (BS, 2 * BS), 1) < BS
    scales = []
    for i in range(rows):
        at = (row_block + i) * NB + col_block
        scales.append(jnp.where(first_lanes, mask[at].astype(F32), mask[at + 1].astype(F32)).astype(dtype))
    return jnp.concatenate(scales, axis=0)


def half_rows(zs):
    return pl.ds(pl.multiple_of((zs & 1) * 2 * BS, 2 * BS), 2 * BS)


def response_kernel(part, idx, mask, *refs):
    groups = ((0, 1, 2), (3,))[part]
    count = 2 * len(groups)
    t_refs, c_own, c_other = refs[:count], refs[count], refs[count + 1]
    before, out, panel = (None, *refs[count + 2:]) if part == 0 else refs[count + 2:]
    x, core, row = idx[0], idx[1], idx[4]
    for g in range(RING):
        panel[(x ^ offset(core, g)) * 2 + core] = c_own[g]
        panel[(x ^ offset(1 - core, g)) * 2 + 1 - core] = c_other[g]
    for v in range(2):
        total = jnp.zeros((4 * BS, 2 * BS), F32) if part == 0 else before[v]
        for k, h in enumerate(groups):
            lefts, rights = [], []
            for g in range(RING):
                ys, zs = source(idx, v, h, g)
                col = ys * RING + zs
                lefts.append(t_refs[v * len(groups) + k][g] * piece_scale(mask, row * 4, col * 2, 4, BF16))
                rights.append(panel[col // 2, half_rows(zs), :])
            total += jnp.dot(
                jnp.concatenate(lefts, axis=1), jnp.concatenate(rights, axis=0), preferred_element_type=F32
            )
        out[v] = total.astype(out.dtype)


def kernel_terms(idx, mask_v, valence, r_panel, flips):
    x, core, z, row = idx[0], idx[1], idx[3], idx[4]
    totals = [[0.0, 0.0], [0.0, 0.0]]
    for slot, flip in enumerate(flips):
        ys = x ^ flip
        for half in range(2):
            lefts, places = [], []
            for g in range(RING):
                zs = z ^ offset(core, g)
                lefts.append(valence(half, ys, g) * piece_scale(mask_v, row * 4 + half * 2, (ys * RING + zs) * 2, 2, BF16))
                places.append(zs)
            left = jnp.concatenate(lefts, axis=1)
            for v in range(2):
                rights = [r_panel[slot * 2 + zs // 2, v, half_rows(zs), :] for zs in places]
                totals[half][v] += jnp.dot(left, jnp.concatenate(rights, axis=0), preferred_element_type=F32)
    return totals


def panel_copies(idx, v_refs, v_panel):
    out = [(v_refs[h], v_panel.at[0, idx[2] ^ offset(idx[1], h)]) for h in range(RING)]
    out += [(v_refs[RING + g], v_panel.at[1, g]) for g in range(RING)]
    return out


def start_all(copies, sems):
    copies = [pltpu.make_async_copy(a, b, sems.at[k]) for k, (a, b) in enumerate(copies)]
    for copy in copies:
        copy.start()
    return copies


def early_kernel(idx, mask_v, *refs):
    v_refs, r_refs, out, v_last, v_panel, r_panel, sems = refs[:8], refs[8:14], *refs[14:]
    core, y = idx[1], idx[2]
    copies = panel_copies(idx, v_refs, v_panel)
    for side in range(2):
        own = core ^ side
        copies.append((r_refs[3 * side], r_panel.at[own]))
        copies.append((r_refs[3 * side + 1], r_panel.at[(1 + own) * 2 + own]))
        copies.append((r_refs[3 * side + 2], r_panel.at[(2 - own) * 2 + own]))
    for copy in start_all(copies, sems):
        copy.wait()

    def valence(half, ys, g):
        return v_panel[0, ys, g] if half == 0 else v_panel[1, g, place_of(core, y ^ ys)]

    for half in range(2):
        for g in range(RING):
            v_last[half, g] = valence(half, idx[0] ^ 2, g)
    totals = kernel_terms(idx, mask_v, valence, r_panel, (0, 1, 3))
    for half in range(2):
        for v in range(2):
            out[v, half * 2 * BS:(half + 1) * 2 * BS, :] = totals[half][v]


def density_kernel(idx, mask, mask_v, starts, *refs):
    v_last, r_own, r_other, before, orb_hbm, near_hbm, far_hbm, k_out, dens, r_panel, orb, partner, sems = refs
    core, row, col = idx[1], idx[4], idx[5]
    copies = [(near_hbm, partner.at[core]), (far_hbm, partner.at[1 - core])]
    copies = start_all(copies + [(orb_hbm.at[i], orb.at[i]) for i in range(4)], sems)
    r_panel[core] = r_own[...]
    r_panel[1 - core] = r_other[...]
    totals = kernel_terms(idx, mask_v, lambda half, ys, g: v_last[half, g], r_panel, (2,))
    for half in range(2):
        scale = piece_scale(mask, row * 4 + half * 2, col * 2, 2, F32)
        rows = slice(half * 2 * BS, (half + 1) * 2 * BS)
        for v in range(2):
            k_out[v, rows, :] = ((before[v, rows, :] + totals[half][v]) * scale).astype(BF16)
    dens[...] = jnp.zeros_like(dens)
    copies[0].wait()
    copies[1].wait()
    starts_j = [starts[col * 2 + j] for j in range(2)]
    for i in range(4):
        copies[2 + i].wait()
        left = jnp.concatenate([k_out[v, i * BS:(i + 1) * BS, :] for v in range(2)], axis=0)
        start_i = starts[row * 4 + i]

        def slabs(step, carry, left=left, start_i=start_i, i=i):
            begin = step * WIDE
            offsets = [start_i + begin - starts_j[j] for j in range(2)]
            touched = [(o > -WIDE) & (o < SPAN) for o in offsets]

            @pl.when(touched[0] | touched[1])
            def _():
                for k in range(WIDE):
                    frames = []
                    for j in range(2):
                        o = offsets[j] + k
                        at = pl.multiple_of(jnp.clip(o, 0, SPAN - 1) * SP, SP)
                        inside = jnp.where((o >= 0) & (o < SPAN), 1.0, 0.0).astype(BF16)
                        frames.append(partner[j, :, pl.ds(at, SP)] * inside)
                    applied = jnp.dot(left, jnp.concatenate(frames, axis=0), preferred_element_type=F32)
                    own = orb[i, :, pl.ds(pl.multiple_of((begin + k) * SP, SP), SP)].astype(F32)
                    for v in range(2):
                        terms = jnp.sum(own * applied[v * BS:(v + 1) * BS], axis=0, keepdims=True)
                        for q in range(4):
                            dens[start_i + begin + k, pl.ds(v * 4 + q, 1), :] += terms[:, q * BS:(q + 1) * BS]

            return carry

        lax.fori_loop(0, SPAN // WIDE, slabs, 0)


SMEM = pl.BlockSpec(memory_space=pltpu.SMEM)
VMEM = pl.BlockSpec(memory_space=pltpu.VMEM)
ANY = pl.BlockSpec(memory_space=pl.ANY)


def local(p_valence, p_conduction, trial_vectors, mask_valence, mask_conduction, mask_trial, orbitals, sphere_starts):
    row, col = lax.axis_index("row"), lax.axis_index("col")
    x, core, y, z = row // 2, row % 2, col // RING, col % RING
    idx = jnp.stack([x, core, y, z, row, col]).astype(jnp.int32)
    mask_flat = mask_trial.reshape(-1)

    first = 2 * (col % 2)
    conduction = masked(p_conduction, mask_conduction, row, col)
    both_z = jnp.concatenate([trial_vectors[0], p_valence[:2 * BS]])
    both_y = jnp.concatenate([trial_vectors[1], p_valence[2 * BS:]])

    mine, theirs = (lax.dynamic_slice_in_dim(orbitals, first + at, 1, 0)[0] for at in (core, 1 - core))
    seed = jnp.where(core == z // 2, mine, send(theirs, OTHER_CORE))
    z_first, y_first, z_second, y_second, seed, conduction = together(
        send(both_z, along("z", 0)), send(both_y, along("y", 0)),
        send(both_z, along("z", 1)), send(both_y, along("y", 1)),
        seed, conduction,
    )
    reached = send(seed, along("x", 0))
    z_third, y_third, x_first, x_second = together(
        send(z_first, along("z", 1)), send(y_first, along("y", 1)), *neighbours(conduction, "x")
    )
    by_z, by_y = [both_z, z_first, z_second, z_third], [both_y, y_first, y_second, y_third]
    own_0 = jnp.stack([piece[:4 * BS] for piece in by_z])
    own_1 = jnp.stack([piece[:4 * BS] for piece in by_y])
    *others, x_third = together(
        *neighbours(own_0, "y"), *neighbours(own_1, "z"), send(x_first, along("x", 1))
    )
    trials_0, trials_1 = [own_0] + others[:2], [own_1] + others[2:]
    trials_0.append(send(trials_0[1], along("y", 1)))
    trials_1.append(send(trials_1[1], along("z", 1)))
    c_own = jnp.stack([conduction, x_first, x_second, x_third])
    c_other = send(c_own, OTHER_CORE)
    passed = jnp.where(x == y, seed, reached)
    arrived = send(passed, along("x", 1))


    response = None
    for part in range(2):
        if part == 1:
            *ends, trials_0[3], trials_1[3], response = together(
                *[piece[4 * BS:] for piece in by_z + by_y], trials_0[3], trials_1[3], response
            )
        groups = (slice(0, 3), slice(3, 4))[part]
        pieces = trials_0[groups] + trials_1[groups]
        response = pl.pallas_call(
            functools.partial(response_kernel, part),
            name="response",
            out_shape=jax.ShapeDtypeStruct((2, 4 * BS, 2 * BS), (F32, BF16)[part]),
            in_specs=[SMEM, SMEM] + [VMEM] * (len(pieces) + 2 + part),
            out_specs=VMEM,
            scratch_shapes=[pltpu.VMEM((8, 4 * BS, 2 * BS), BF16)],
            compiler_params=pltpu.CompilerParams(vmem_limit_bytes=24 * 2**20),
            cost_estimate=pl.CostEstimate(flops=2**(32 + 4 * part), bytes_accessed=9 * 2**20, transcendentals=0),
        )(idx, mask_flat, *pieces, c_own, c_other, *([response] if part else []))

    valences = [jnp.stack(ends[:4]), jnp.stack(ends[4:8])]
    valences = [valences[0], send(valences[0], along("y", 0)), valences[1], send(valences[1], along("z", 0))]
    responses = [response, *neighbours(response, "x"), None]
    valences = [
        valences[0], valences[1], send(valences[0], along("y", 1)), send(valences[1], along("y", 1)),
        valences[2], valences[3], send(valences[2], along("z", 1)), send(valences[3], along("z", 1)),
    ]
    *valences, responses[1], responses[2], arrived = together(*valences, *responses[1:3], arrived)
    responses[3] = send(responses[1], along("x", 1))
    swapped = [send(piece, OTHER_CORE) for piece in responses[:3]]
    near = jnp.where((x == y) | (x ^ (1 + 2 * core) == y), passed, arrived)
    far = send(near, OTHER_CORE)
    mask_v = mask_valence.reshape(-1)

    early, v_last = pl.pallas_call(
        early_kernel,
        name="early",
        out_shape=(
            jax.ShapeDtypeStruct((2, 4 * BS, 2 * BS), F32),
            jax.ShapeDtypeStruct((2, RING, 2 * BS, 2 * BS), BF16),
        ),
        in_specs=[SMEM, SMEM] + [ANY] * 14,
        out_specs=(VMEM, VMEM),
        scratch_shapes=[
            pltpu.VMEM((2, RING, RING, 2 * BS, 2 * BS), BF16),
            pltpu.VMEM((6, 2, 4 * BS, 2 * BS), BF16),
            pltpu.SemaphoreType.DMA((14,)),
        ],
        compiler_params=pltpu.CompilerParams(vmem_limit_bytes=20 * 2**20),
        cost_estimate=pl.CostEstimate(flops=2**36, bytes_accessed=8 * 2**20, transcendentals=0),
    )(idx, mask_v, *valences, *responses[:3], *swapped[:3])

    responses[3], early = together(responses[3], early)
    swapped.append(send(responses[3], OTHER_CORE))

    kernel, density = pl.pallas_call(
        density_kernel,
        name="density",
        out_shape=(
            jax.ShapeDtypeStruct((2, 4 * BS, 2 * BS), BF16),
            jax.ShapeDtypeStruct((NSLAB, 8, BS), F32),
        ),
        in_specs=[SMEM] * 4 + [VMEM] * 4 + [ANY] * 3,
        out_specs=(VMEM, VMEM),
        scratch_shapes=[
            pltpu.VMEM((2, 2, 4 * BS, 2 * BS), BF16),
            pltpu.VMEM((4, BS, SPAN * SP), BF16),
            pltpu.VMEM((2, BS, SPAN * SP), BF16),
            pltpu.SemaphoreType.DMA((6,)),
        ],
        compiler_params=pltpu.CompilerParams(vmem_limit_bytes=28 * 2**20),
        cost_estimate=pl.CostEstimate(flops=2**33, bytes_accessed=22 * 2**20, transcendentals=0),
    )(idx, mask_flat, mask_v, sphere_starts, v_last, responses[3], swapped[3], early, orbitals, near, far)

    terms = lax.all_to_all(density, AXES, 0, 0, tiled=True)
    return kernel, jnp.sum(terms, axis=0).reshape(2, SP)


def solution(mesh):
    placed = (
        P("row", "col"),
        P("row", "col"),
        P(None, "row", "col"),
        P(),
        P(),
        P(),
        P("row", None, None),
        P(),
    )
    return jax.shard_map(
        local,
        mesh=mesh,
        in_specs=placed,
        out_specs=(P(None, "row", "col"), P(None, AXES)),
        check_vma=False,
    )
```

```python
import functools

import jax
import jax.numpy as jnp
from jax import lax
from jax.experimental import pallas as pl
from jax.experimental.pallas import tpu as pltpu
from jax.sharding import PartitionSpec as P

BS = 128
NB = 32
SPAN = 16
SP = 512
NSLAB = 128
RING = 4
N_COL = 16
WIDE = 4
BF16 = jnp.bfloat16
F32 = jnp.float32
AXES = ("row", "col")


def place(x, core, y, z):
    return ((x % RING) * 2 + core) * N_COL + (y % RING) * RING + z % RING


def pairs(move):
    out = []
    for x in range(RING):
        for core in range(2):
            for y in range(RING):
                for z in range(RING):
                    target = move(x, core, y, z)
                    if target is not None:
                        out.append((place(x, core, y, z), place(*target)))
    return out


def along(axis, step):
    def move(x, core, y, z, flip):
        at = [x, y, z]
        at["xyz".index(axis)] ^= flip
        return at[0], core, at[1], at[2]

    return pairs(lambda x, core, y, z: move(x, core, y, z, 1 if core == step else 3))


OTHER_CORE = pairs(lambda x, core, y, z: (x, 1 - core, y, z))

def send(value, route):
    return lax.ppermute(value, AXES, route)


def together(*values):
    return lax.optimization_barrier(values)


def neighbours(value, axis):
    return [send(value, along(axis, 0)), send(value, along(axis, 1))]


def gather(value, axis):
    first, second = neighbours(value, axis)
    return [value, first, second, send(first, along(axis, 1))]


def masked(values, block_mask, row_index, col_index):
    row_blocks, col_blocks = values.shape[0] // BS, values.shape[1] // BS
    tile_mask = lax.dynamic_slice(
        block_mask, (row_index * row_blocks, col_index * col_blocks), (row_blocks, col_blocks)
    ).astype(values.dtype)
    shaped = values.reshape(row_blocks, BS, col_blocks, BS)
    return (shaped * tile_mask[:, None, :, None]).reshape(values.shape)


def offset(core, g):
    return (0, 1 + 2 * core, 3 - 2 * core, 2)[g]


def source(idx, first, h, g):
    dy, dz = (h, g) if first == 0 else (g, h)
    return idx[2] ^ offset(idx[1], dy), idx[3] ^ offset(idx[1], dz)


def place_of(core, flip):
    return jnp.where(flip == 2, 3, jnp.where(flip == 0, 0, jnp.where(flip == 1 + 2 * core, 1, 2)))


def piece_scale(mask, row_block, col_block, rows, dtype):
    first_lanes = lax.broadcasted_iota(jnp.int32, (BS, 2 * BS), 1) < BS
    scales = []
    for i in range(rows):
        at = (row_block + i) * NB + col_block
        scales.append(jnp.where(first_lanes, mask[at].astype(F32), mask[at + 1].astype(F32)).astype(dtype))
    return jnp.concatenate(scales, axis=0)


def half_rows(zs):
    return pl.ds(pl.multiple_of((zs & 1) * 2 * BS, 2 * BS), 2 * BS)


def response_kernel(part, idx, mask, *refs):
    groups = ((0, 1, 2), (3,))[part]
    count = 2 * len(groups)
    t_refs, c_own, c_other = refs[:count], refs[count], refs[count + 1]
    before, out, panel = (None, *refs[count + 2:]) if part == 0 else refs[count + 2:]
    x, core, row = idx[0], idx[1], idx[4]
    for g in range(RING):
        panel[(x ^ offset(core, g)) * 2 + core] = c_own[g]
        panel[(x ^ offset(1 - core, g)) * 2 + 1 - core] = c_other[g]
    for v in range(2):
        total = jnp.zeros((4 * BS, 2 * BS), F32) if part == 0 else before[v]
        for k, h in enumerate(groups):
            lefts, rights = [], []
            for g in range(RING):
                ys, zs = source(idx, v, h, g)
                col = ys * RING + zs
                lefts.append(t_refs[v * len(groups) + k][g] * piece_scale(mask, row * 4, col * 2, 4, BF16))
                rights.append(panel[col // 2, half_rows(zs), :])
            total += jnp.dot(
                jnp.concatenate(lefts, axis=1), jnp.concatenate(rights, axis=0), preferred_element_type=F32
            )
        out[v] = total.astype(out.dtype)


def kernel_terms(idx, mask_v, valence, r_panel, flips):
    x, core, z, row = idx[0], idx[1], idx[3], idx[4]
    totals = [[0.0, 0.0], [0.0, 0.0]]
    for slot, flip in enumerate(flips):
        ys = x ^ flip
        for half in range(2):
            lefts, places = [], []
            for g in range(RING):
                zs = z ^ offset(core, g)
                lefts.append(valence(half, ys, g) * piece_scale(mask_v, row * 4 + half * 2, (ys * RING + zs) * 2, 2, BF16))
                places.append(zs)
            left = jnp.concatenate(lefts, axis=1)
            for v in range(2):
                rights = [r_panel[slot * 2 + zs // 2, v, half_rows(zs), :] for zs in places]
                totals[half][v] += jnp.dot(left, jnp.concatenate(rights, axis=0), preferred_element_type=F32)
    return totals


def panel_copies(idx, v_refs, v_panel):
    out = [(v_refs[h], v_panel.at[0, idx[2] ^ offset(idx[1], h)]) for h in range(RING)]
    out += [(v_refs[RING + g], v_panel.at[1, g]) for g in range(RING)]
    return out


def start_all(copies, sems):
    copies = [pltpu.make_async_copy(a, b, sems.at[k]) for k, (a, b) in enumerate(copies)]
    for copy in copies:
        copy.start()
    return copies


def early_kernel(idx, mask_v, *refs):
    v_refs, r_refs, out, v_last, v_panel, r_panel, sems = refs[:8], refs[8:14], *refs[14:]
    core, y = idx[1], idx[2]
    copies = panel_copies(idx, v_refs, v_panel)
    for side in range(2):
        own = core ^ side
        copies.append((r_refs[3 * side], r_panel.at[own]))
        copies.append((r_refs[3 * side + 1], r_panel.at[(1 + own) * 2 + own]))
        copies.append((r_refs[3 * side + 2], r_panel.at[(2 - own) * 2 + own]))
    for copy in start_all(copies, sems):
        copy.wait()

    def valence(half, ys, g):
        return v_panel[0, ys, g] if half == 0 else v_panel[1, g, place_of(core, y ^ ys)]

    for half in range(2):
        for g in range(RING):
            v_last[half, g] = valence(half, idx[0] ^ 2, g)
    totals = kernel_terms(idx, mask_v, valence, r_panel, (0, 1, 3))
    for half in range(2):
        for v in range(2):
            out[v, half * 2 * BS:(half + 1) * 2 * BS, :] = totals[half][v]


def density_kernel(idx, mask, mask_v, starts, *refs):
    v_last, r_own, r_other, before, orb_hbm, near_hbm, far_hbm, k_out, dens, r_panel, orb, partner, sems = refs
    core, row, col = idx[1], idx[4], idx[5]
    copies = [(near_hbm, partner.at[core]), (far_hbm, partner.at[1 - core])]
    copies = start_all(copies + [(orb_hbm.at[i], orb.at[i]) for i in range(4)], sems)
    r_panel[core] = r_own[...]
    r_panel[1 - core] = r_other[...]
    totals = kernel_terms(idx, mask_v, lambda half, ys, g: v_last[half, g], r_panel, (2,))
    for half in range(2):
        scale = piece_scale(mask, row * 4 + half * 2, col * 2, 2, F32)
        rows = slice(half * 2 * BS, (half + 1) * 2 * BS)
        for v in range(2):
            k_out[v, rows, :] = ((before[v, rows, :] + totals[half][v]) * scale).astype(BF16)
    dens[...] = jnp.zeros_like(dens)
    copies[0].wait()
    copies[1].wait()
    starts_j = [starts[col * 2 + j] for j in range(2)]
    for i in range(4):
        copies[2 + i].wait()
        left = jnp.concatenate([k_out[v, i * BS:(i + 1) * BS, :] for v in range(2)], axis=0)
        start_i = starts[row * 4 + i]

        def slabs(step, carry, left=left, start_i=start_i, i=i):
            begin = step * WIDE
            offsets = [start_i + begin - starts_j[j] for j in range(2)]
            touched = [(o > -WIDE) & (o < SPAN) for o in offsets]

            @pl.when(touched[0] | touched[1])
            def _():
                for k in range(WIDE):
                    frames = []
                    for j in range(2):
                        o = offsets[j] + k
                        at = pl.multiple_of(jnp.clip(o, 0, SPAN - 1) * SP, SP)
                        inside = jnp.where((o >= 0) & (o < SPAN), 1.0, 0.0).astype(BF16)
                        frames.append(partner[j, :, pl.ds(at, SP)] * inside)
                    applied = jnp.dot(left, jnp.concatenate(frames, axis=0), preferred_element_type=F32)
                    own = orb[i, :, pl.ds(pl.multiple_of((begin + k) * SP, SP), SP)].astype(F32)
                    for v in range(2):
                        terms = jnp.sum(own * applied[v * BS:(v + 1) * BS], axis=0, keepdims=True)
                        for q in range(4):
                            dens[start_i + begin + k, pl.ds(v * 4 + q, 1), :] += terms[:, q * BS:(q + 1) * BS]

            return carry

        lax.fori_loop(0, SPAN // WIDE, slabs, 0)


SMEM = pl.BlockSpec(memory_space=pltpu.SMEM)
VMEM = pl.BlockSpec(memory_space=pltpu.VMEM)
ANY = pl.BlockSpec(memory_space=pl.ANY)


def local(p_valence, p_conduction, trial_vectors, mask_valence, mask_conduction, mask_trial, orbitals, sphere_starts):
    row, col = lax.axis_index("row"), lax.axis_index("col")
    x, core, y, z = row // 2, row % 2, col // RING, col % RING
    idx = jnp.stack([x, core, y, z, row, col]).astype(jnp.int32)
    mask_flat = mask_trial.reshape(-1)

    first = 2 * (col % 2)
    conduction = masked(p_conduction, mask_conduction, row, col)
    both_z = jnp.concatenate([trial_vectors[0], p_valence[:2 * BS]])
    both_y = jnp.concatenate([trial_vectors[1], p_valence[2 * BS:]])

    mine, theirs = (lax.dynamic_slice_in_dim(orbitals, first + at, 1, 0)[0] for at in (core, 1 - core))
    seed = jnp.where(core == z // 2, mine, send(theirs, OTHER_CORE))
    z_first, y_first, z_second, y_second, seed, conduction = together(
        send(both_z, along("z", 0)), send(both_y, along("y", 0)),
        send(both_z, along("z", 1)), send(both_y, along("y", 1)),
        seed, conduction,
    )
    reached = send(seed, along("x", 0))
    z_third, y_third, x_first, x_second = together(
        send(z_first, along("z", 1)), send(y_first, along("y", 1)), *neighbours(conduction, "x")
    )
    by_z, by_y = [both_z, z_first, z_second, z_third], [both_y, y_first, y_second, y_third]
    own_0 = jnp.stack([piece[:4 * BS] for piece in by_z])
    own_1 = jnp.stack([piece[:4 * BS] for piece in by_y])
    *others, x_third = together(
        *neighbours(own_0, "y"), *neighbours(own_1, "z"), send(x_first, along("x", 1))
    )
    trials_0, trials_1 = [own_0] + others[:2], [own_1] + others[2:]
    trials_0.append(send(trials_0[1], along("y", 1)))
    trials_1.append(send(trials_1[1], along("z", 1)))
    c_own = jnp.stack([conduction, x_first, x_second, x_third])
    c_other = send(c_own, OTHER_CORE)
    passed = jnp.where(x == y, seed, reached)
    arrived = send(passed, along("x", 1))


    response = None
    for part in range(2):
        if part == 1:
            *ends, trials_0[3], trials_1[3], response = together(
                *[piece[4 * BS:] for piece in by_z + by_y], trials_0[3], trials_1[3], response
            )
        groups = (slice(0, 3), slice(3, 4))[part]
        pieces = trials_0[groups] + trials_1[groups]
        response = pl.pallas_call(
            functools.partial(response_kernel, part),
            name="response",
            out_shape=jax.ShapeDtypeStruct((2, 4 * BS, 2 * BS), (F32, BF16)[part]),
            in_specs=[SMEM, SMEM] + [VMEM] * (len(pieces) + 2 + part),
            out_specs=VMEM,
            scratch_shapes=[pltpu.VMEM((8, 4 * BS, 2 * BS), BF16)],
            compiler_params=pltpu.CompilerParams(vmem_limit_bytes=24 * 2**20),
            cost_estimate=pl.CostEstimate(flops=2**(32 + 4 * part), bytes_accessed=9 * 2**20, transcendentals=0),
        )(idx, mask_flat, *pieces, c_own, c_other, *([response] if part else []))

    valences = [jnp.stack(ends[:4]), jnp.stack(ends[4:8])]
    valences = [valences[0], send(valences[0], along("y", 0)), valences[1], send(valences[1], along("z", 0))]
    responses = [response, *neighbours(response, "x"), None]
    valences = [
        valences[0], valences[1], send(valences[0], along("y", 1)), send(valences[1], along("y", 1)),
        valences[2], valences[3], send(valences[2], along("z", 1)), send(valences[3], along("z", 1)),
    ]
    *valences, responses[1], responses[2], arrived = together(*valences, *responses[1:3], arrived)
    responses[3] = send(responses[1], along("x", 1))
    swapped = [send(piece, OTHER_CORE) for piece in responses[:3]]
    near = jnp.where((x == y) | (x ^ (1 + 2 * core) == y), passed, arrived)
    far = send(near, OTHER_CORE)
    mask_v = mask_valence.reshape(-1)

    early, v_last = pl.pallas_call(
        early_kernel,
        name="early",
        out_shape=(
            jax.ShapeDtypeStruct((2, 4 * BS, 2 * BS), F32),
            jax.ShapeDtypeStruct((2, RING, 2 * BS, 2 * BS), BF16),
        ),
        in_specs=[SMEM, SMEM] + [ANY] * 14,
        out_specs=(VMEM, VMEM),
        scratch_shapes=[
            pltpu.VMEM((2, RING, RING, 2 * BS, 2 * BS), BF16),
            pltpu.VMEM((6, 2, 4 * BS, 2 * BS), BF16),
            pltpu.SemaphoreType.DMA((14,)),
        ],
        compiler_params=pltpu.CompilerParams(vmem_limit_bytes=20 * 2**20),
        cost_estimate=pl.CostEstimate(flops=2**36, bytes_accessed=8 * 2**20, transcendentals=0),
    )(idx, mask_v, *valences, *responses[:3], *swapped[:3])

    responses[3], early = together(responses[3], early)
    swapped.append(send(responses[3], OTHER_CORE))

    kernel, density = pl.pallas_call(
        density_kernel,
        name="density",
        out_shape=(
            jax.ShapeDtypeStruct((2, 4 * BS, 2 * BS), BF16),
            jax.ShapeDtypeStruct((NSLAB, 8, BS), F32),
        ),
        in_specs=[SMEM] * 4 + [VMEM] * 4 + [ANY] * 3,
        out_specs=(VMEM, VMEM),
        scratch_shapes=[
            pltpu.VMEM((2, 2, 4 * BS, 2 * BS), BF16),
            pltpu.VMEM((4, BS, SPAN * SP), BF16),
            pltpu.VMEM((2, BS, SPAN * SP), BF16),
            pltpu.SemaphoreType.DMA((6,)),
        ],
        compiler_params=pltpu.CompilerParams(vmem_limit_bytes=28 * 2**20),
        cost_estimate=pl.CostEstimate(flops=2**33, bytes_accessed=22 * 2**20, transcendentals=0),
    )(idx, mask_flat, mask_v, sphere_starts, v_last, responses[3], swapped[3], early, orbitals, near, far)

    terms = lax.all_to_all(density, AXES, 0, 0, tiled=True)
    return kernel, jnp.sum(terms, axis=0).reshape(2, SP)


def solution(mesh):
    placed = (
        P("row", "col"),
        P("row", "col"),
        P(None, "row", "col"),
        P(),
        P(),
        P(),
        P("row", None, None),
        P(),
    )
    return jax.shard_map(
        local,
        mesh=mesh,
        in_specs=placed,
        out_specs=(P(None, "row", "col"), P(None, AXES)),
        check_vma=False,
    )
```
